32 devices in a mesh: chan: 16 (over z, x, core), img: 2 (over y).
Axes of the slice: x: 2, y: 2, z: 4, core: 2. Of those that a mesh axis runs over, the one named last changes fastest.
Arguments:
- tokens: bfloat16 [32, 512, 1024], P('chan', 'img'), may hold values from -6 to 6
- chan_embed: float32 [32, 1024], P('chan'), may hold values from -6 to 6
- value_proj: bfloat16 [1024, 1024], replicated, may hold values from -0.1875 to 0.1875
- key_query: bfloat16 [1024, 16], replicated, may hold values from -0.1875 to 0.1875
- chan_bias: float32 [32, 16], replicated, may hold values from -5 to 400
- cotangent: bfloat16 [512, 1024], P(('img', 'chan')), may hold values from -96 to 96
Outputs:
- grad_input: bfloat16 [32, 512, 1024], P('chan', 'img')
- grad_embed: float32 [32, 1024], P('chan')
- grad_bias: float32 [32, 16], P('chan')
The draws below stay inside these ranges and needn't reach their ends.
All inputs are finite; a program needn't handle non-finite values.
Results may differ from the reference program's by a relative error of at most 0.007.
Values may be sent and summed in bfloat16 or wider, within the bound.
A program may use at most 64 MiB of HBM per device.

```python
import jax
import jax.numpy as jnp
from jax import lax

D = 1024
H = 16
CHANNELS = 32
TOKENS = 512
N_IMG = 2


def draw_chan_bias(key, part):
    key_base = jax.random.fold_in(key, 0)
    return jnp.clip(jax.random.normal(key_base, (CHANNELS, H), jnp.float32), -5.0, 5.0)


def steps_of(stream_key, extent, cuts, least, top_value):
    loudness = 1.0
    for axis_at, parts in cuts:
        steps = jax.random.uniform(jax.random.fold_in(jax.random.fold_in(stream_key, 6), axis_at), (parts,), jnp.float32, least / len(cuts), top_value / len(cuts))
        loudness = loudness * jnp.repeat(jnp.exp(steps), extent[axis_at] // parts).reshape((-1,) + (1,) * (len(extent) - 1 - axis_at))
    return loudness


def noise(stream_key, shape, deviation, reach, cuts=(), kind=jnp.bfloat16):
    loudness = steps_of(stream_key, shape, cuts, -0.22, 0.18) if cuts else 1.0
    entries = jax.random.normal(stream_key, shape, jnp.float32) * deviation * loudness
    return jnp.minimum(jnp.maximum(entries, -reach), reach).astype(kind)


def setup_inputs(seed: int = 0) -> dict:
    streams_of = jax.random.split(jax.random.key(seed), 7)
    tokens = noise(streams_of[0], (CHANNELS, TOKENS, D), 1.0, 6.0, ((0, 16), (1, 2)))
    chan_embed = noise(streams_of[1], (CHANNELS, D), 1.0, 6.0, ((0, 16),), jnp.float32)
    value_proj = noise(streams_of[2], (D, D), D ** -0.5, 0.1875)
    key_query = noise(streams_of[3], (D, H), D ** -0.5, 0.1875)
    chan_bias = draw_chan_bias(jax.random.fold_in(streams_of[6], 71), 0)
    cotangent = noise(streams_of[5], (TOKENS, D), 16.0, 96.0, ((0, 32),))
    return dict(tokens=tokens, chan_embed=chan_embed, value_proj=value_proj, key_query=key_query, chan_bias=chan_bias, cotangent=cotangent)


def block_grads(shifted, grad_rows, value_proj, key_query, chan_bias):
    num_chans, num_rows, model_width = shifted.shape
    num_heads = key_query.shape[1]
    flat_rows = shifted.reshape(num_chans * num_rows, model_width)
    values = jnp.dot(flat_rows, value_proj, preferred_element_type=jnp.float32).astype(jnp.bfloat16)
    values = values.reshape(num_chans, num_rows, num_heads, model_width // num_heads)
    scores = jnp.dot(flat_rows, key_query, preferred_element_type=jnp.float32).reshape(num_chans, num_rows, num_heads)
    scores = scores + chan_bias[:, None, :]
    soft_weights = jax.nn.softmax(scores, axis=0)
    grad_heads = grad_rows.reshape(num_rows, num_heads, model_width // num_heads)
    prob_grad = jnp.einsum("cthk,thk->cth", values.astype(jnp.float32), grad_heads.astype(jnp.float32))
    score_grad = soft_weights * (prob_grad - jnp.sum(soft_weights * prob_grad, axis=0, keepdims=True))
    value_grad = (soft_weights[..., None] * grad_heads.astype(jnp.float32)[None]).astype(jnp.bfloat16)
    value_grad = value_grad.reshape(num_chans * num_rows, model_width)
    score_grad_b = score_grad.astype(jnp.bfloat16).reshape(num_chans * num_rows, num_heads)
    grad_sum = jnp.dot(value_grad, value_proj.T, preferred_element_type=jnp.float32)
    grad_sum = grad_sum + jnp.dot(score_grad_b, key_query.T, preferred_element_type=jnp.float32)
    grad_input = grad_sum.astype(jnp.bfloat16).reshape(num_chans, num_rows, model_width)
    return grad_input, jnp.sum(grad_input.astype(jnp.float32), axis=1), jnp.sum(score_grad, axis=1)


def reference(tokens, chan_embed, value_proj, key_query, chan_bias, cotangent):
    shifted = (tokens.astype(jnp.float32) + chan_embed[:, None, :]).astype(jnp.bfloat16)
    num_blocks = N_IMG
    num_rows = TOKENS // num_blocks
    shifted_blocks = shifted.reshape(CHANNELS, num_blocks, num_rows, D).transpose(1, 0, 2, 3)
    grad_blocks = cotangent.reshape(num_blocks, num_rows, D)

    def one_block(pair):
        return block_grads(pair[0], pair[1], value_proj, key_query, chan_bias)

    grad_parts, embed_parts, bias_parts = lax.map(one_block, (shifted_blocks, grad_blocks))
    grad_input = grad_parts.transpose(1, 0, 2, 3).reshape(CHANNELS, TOKENS, D)
    return grad_input, jnp.sum(embed_parts, axis=0), jnp.sum(bias_parts, axis=0)
```

```python
import functools

import jax
import jax.numpy as jnp
from jax import lax
from jax.experimental import pallas as pl
from jax.experimental.pallas import tpu as pltpu
from jax.sharding import PartitionSpec as P

MESH = pl.DeviceIdType.MESH
F32 = jnp.float32
BF16 = jnp.bfloat16
ROWS_BY_ROWS = (((1,), (1,)), ((), ()))


def dot_t(left, right):
    return lax.dot_general(left, right, ROWS_BY_ROWS, preferred_element_type=F32)


def dot(left, right):
    return jnp.dot(left, right, preferred_element_type=F32)


def grid_of(n):
    chips = n // 2
    wide = 1
    while wide * wide * 4 <= chips:
        wide *= 2
    return chips // wide, wide


def kernel(
    n, g, gather,
    tokens, embed, proj, query, bias, cot,
    out_grad, out_embed, out_bias,
    tok, emb, pv, kq, bia, cots, shifted, values, vgrad, outv, oemb, obias,
    stat_out, stat_in, tot_out, tot_in, img_out, img_in,
    load_sem, store_sem, cot_send, cot_recv, stat_send, stat_recv, tot_send, tot_recv,
    img_send, img_recv,
):
    chans, toks, width = tokens.shape
    heads = query.shape[1]
    depth = width // heads
    tile = min(256, width)
    tiles = width // tile
    me = lax.axis_index("chan")
    my_img = lax.axis_index("img")
    rows = cot.shape[0]

    def load(slot, src, dst):
        copy = pltpu.make_async_copy(src, dst, load_sem.at[slot])
        copy.start()
        return copy

    if gather:
        cot_load = load(0, cot, cots.at[pl.ds(pl.multiple_of(me * rows, rows), rows)])
    else:
        cot_load = load(0, cot, cots)
    small_loads = [load(1, embed, emb), load(2, bias, bia), load(3, query, kq)]
    tok_loads = [load(4 + c, tokens.at[c], tok.at[pl.ds(c * toks, toks)]) for c in range(chans)]
    proj_loads = [
        load(
            4 + chans + j,
            proj.at[:, pl.ds(j * tile, tile)],
            pv.at[:, pl.ds(j * tile, tile)],
        )
        for j in range(tiles)
    ]

    barrier = pltpu.get_barrier_semaphore()
    for k in range(1, n):
        pl.semaphore_signal(
            barrier, inc=1, device_id={"chan": lax.rem(me + k, n)}, device_id_type=MESH
        )
    for k in range(1, g):
        pl.semaphore_signal(
            barrier, inc=1, device_id={"img": lax.rem(my_img + k, g)}, device_id_type=MESH
        )
    pl.semaphore_wait(barrier, n - 1 + g - 1)

    tall, wide = grid_of(n)
    core = lax.rem(me, 2)
    my_b = lax.rem(me // 2, wide)
    my_a = me // (2 * wide)

    def index(a, b, c):
        return (a * wide + b) * 2 + c

    sends = []

    def block(i):
        return cots.at[pl.ds(pl.multiple_of(i * rows, rows), rows)]

    def send(i, to, own=False):
        copy = pltpu.make_async_remote_copy(
            src_ref=cot if own else block(i),
            dst_ref=block(i),
            send_sem=cot_send.at[len(sends)],
            recv_sem=cot_recv.at[i],
            device_id={"chan": to},
            device_id_type=MESH,
        )
        copy.start()
        sends.append(copy)

    def arrive(i):
        pltpu.make_async_remote_copy(
            src_ref=cot,
            dst_ref=block(i),
            send_sem=cot_send.at[0],
            recv_sem=cot_recv.at[i],
            device_id={"chan": me},
            device_id_type=MESH,
        ).wait_recv()

    def others_a():
        return [lax.rem(my_a + k, tall) for k in range(1, tall)]

    def others_b():
        return [lax.rem(my_b + k, wide) for k in range(1, wide)]

    mate = index(my_a, my_b, 1 - core)
    if gather:
        for a in others_a():
            send(me, index(a, my_b, core), own=True)
        for b in others_b():
            send(me, index(my_a, b, core), own=True)
        send(me, mate, own=True)

    for copy in small_loads:
        copy.wait()
    kq_t = kq[...].astype(F32).T.astype(BF16)
    head_at = lax.broadcasted_iota(jnp.int32, (heads, width), 0) * depth
    lane_at = lax.broadcasted_iota(jnp.int32, (heads, width), 1)
    spread_f = jnp.where((lane_at >= head_at) & (lane_at < head_at + depth), 1.0, 0.0)
    spread = spread_f.astype(BF16)
    eye = lax.broadcasted_iota(jnp.int32, (heads, 128), 0) == lax.broadcasted_iota(
        jnp.int32, (heads, 128), 1
    )
    small_eye = lax.broadcasted_iota(jnp.int32, (heads, heads), 0) == lax.broadcasted_iota(
        jnp.int32, (heads, heads), 1
    )

    scores = []
    for c in range(chans):
        tok_loads[c].wait()
        at = pl.ds(c * toks, toks)
        moved = (tok[at, :].astype(F32) + emb[pl.ds(c, 1), :]).astype(BF16)
        shifted[at, :] = moved
        bias_row = bia[pl.ds(me * chans + c, 1), :]
        bias_col = jnp.sum(jnp.where(small_eye, bias_row, 0.0), axis=1, keepdims=True)
        scores.append(dot_t(kq_t, moved) + bias_col)

    def value_tile(j):
        proj_loads[j].wait()
        cols = pl.ds(j * tile, tile)
        values[:, cols] = dot(shifted[...], pv[:, cols]).astype(BF16)

    peak = functools.reduce(jnp.maximum, scores)
    exps = [jnp.exp(s - peak) for s in scores]
    exp_sum = functools.reduce(jnp.add, exps)

    done = 0
    if gather:
        steps = []
        for a in others_a():
            def forward(a=a):
                i = index(a, my_b, core)
                arrive(i)
                for b in others_b():
                    send(i, index(my_a, b, core))
                send(i, mate)
            steps.append(forward)
        for b in others_b():
            for k in range(tall):
                def pass_on(b=b, k=k):
                    i = index(lax.rem(my_a + k, tall), b, core)
                    arrive(i)
                    send(i, mate)
                steps.append(pass_on)
        value_tile(0)
        done = 1
        per_tile = -(-len(steps) // max(1, tiles - 1))
        at_step = 0
        while at_step < len(steps):
            for step in steps[at_step:at_step + per_tile]:
                step()
            at_step += per_tile
            if done < tiles:
                value_tile(done)
                done += 1
    while done < tiles:
        value_tile(done)
        done += 1
    cot_load.wait()
    if gather:
        for a in range(tall):
            for b in range(wide):
                arrive(index(a, b, 1 - core))

    cot_rows = cots[...]
    prob = []
    for c in range(chans):
        at = pl.ds(c * toks, toks)
        prob.append(dot_t(spread, values[at, :] * cot_rows))
    weighted = functools.reduce(jnp.add, [e * p for e, p in zip(exps, prob)])
    stat_out[:, 0, :] = peak
    stat_out[:, 1, :] = exp_sum
    stat_out[:, 2, :] = weighted

    stat_sends = []
    for k in range(1, n):
        to = lax.rem(me + k, n)
        copy = pltpu.make_async_remote_copy(
            src_ref=stat_out.at[lax.rem(to, heads)],
            dst_ref=stat_in.at[me],
            send_sem=stat_send.at[k],
            recv_sem=stat_recv.at[me],
            device_id={"chan": to},
            device_id_type=MESH,
        )
        stat_sends.append(copy)

        @pl.when(to < heads)
        def _(copy=copy):
            copy.start()

    def exchange_totals():
        stat_in[me] = stat_out[lax.rem(me, heads)]
        for k in range(1, n):
            frm = lax.rem(me + k, n)
            pltpu.make_async_remote_copy(
                src_ref=stat_out.at[0],
                dst_ref=stat_in.at[frm],
                send_sem=stat_send.at[0],
                recv_sem=stat_recv.at[frm],
                device_id={"chan": me},
                device_id_type=MESH,
            ).wait_recv()
        peaks = stat_in[:, 0, :]
        top = jnp.max(peaks, axis=0, keepdims=True)
        scale = jnp.exp(peaks - top)
        total = jnp.sum(stat_in[:, 1, :] * scale, axis=0, keepdims=True)
        mean = jnp.sum(stat_in[:, 2, :] * scale, axis=0, keepdims=True) / total
        tot_out[0:1, :] = top
        tot_out[1:2, :] = 1.0 / total
        tot_out[2:3, :] = mean
        copies = []
        for k in range(1, n):
            copy = pltpu.make_async_remote_copy(
                src_ref=tot_out,
                dst_ref=tot_in.at[lax.rem(me, heads)],
                send_sem=tot_send.at[k],
                recv_sem=tot_recv.at[lax.rem(me, heads)],
                device_id={"chan": lax.rem(me + k, n)},
                device_id_type=MESH,
            )
            copy.start()
            copies.append(copy)
        tot_in[lax.rem(me, heads)] = tot_out[...]
        for copy in copies:
            copy.wait_send()

    if n == heads:
        exchange_totals()
    else:
        pl.when(me < heads)(exchange_totals)

    def total_arrives(h):
        pltpu.make_async_remote_copy(
            src_ref=tot_out,
            dst_ref=tot_in.at[h],
            send_sem=tot_send.at[0],
            recv_sem=tot_recv.at[h],
            device_id={"chan": me},
            device_id_type=MESH,
        ).wait_recv()

    if n == heads:
        for k in range(1, n):
            total_arrives(lax.rem(me + k, n))
    else:
        for h in range(heads):
            pl.when(me != h)(functools.partial(total_arrives, h))

    top = tot_in[:, 0, :]
    inverse = tot_in[:, 1, :]
    mean = tot_in[:, 2, :]

    zeros = jnp.zeros((heads, width), BF16)
    spread3 = jnp.concatenate([spread, spread, zeros], axis=0)
    query3 = jnp.concatenate([zeros, zeros, kq_t], axis=0)
    cot_f = cot_rows.astype(F32)
    mixes = []
    for c in range(chans):
        soft = jnp.exp(scores[c] - top) * inverse
        score_grad = soft * (prob[c] - mean)
        high = soft.astype(BF16).astype(F32)
        mix = jnp.concatenate([high, soft - high, score_grad], axis=0).T.astype(BF16)
        mixes.append(mix)
        grad = (dot(mix, spread3) * cot_f).astype(BF16)
        vgrad[pl.ds(c * toks, toks), :] = grad
        img_out[pl.ds(c, 1), :width] = jnp.sum(grad.astype(F32), axis=0, keepdims=True)
        bias_sum = jnp.sum(score_grad, axis=1, keepdims=True)
        img_out[pl.ds(c, 1), width:] = jnp.sum(jnp.where(eye, bias_sum, 0.0), axis=0, keepdims=True)

    img_copies = []
    for k in range(1, g):
        copy = pltpu.make_async_remote_copy(
            src_ref=img_out,
            dst_ref=img_in.at[k - 1],
            send_sem=img_send.at[k],
            recv_sem=img_recv.at[k],
            device_id={"img": lax.rem(my_img + k, g)},
            device_id_type=MESH,
        )
        copy.start()
        img_copies.append(copy)

    stores = []
    for j in range(tiles):
        cols = pl.ds(j * tile, tile)
        acc = dot_t(vgrad[...], pv[cols, :])
        mine = jnp.concatenate([dot(mix, query3[:, j * tile:(j + 1) * tile]) for mix in mixes], axis=0)
        outv[:, cols] = (acc + mine).astype(BF16)
        for c in range(chans):
            copy = pltpu.make_async_copy(
                outv.at[pl.ds(c * toks, toks), cols],
                out_grad.at[c, :, cols],
                store_sem.at[j * chans + c],
            )
            copy.start()
            stores.append(copy)

    sums = img_out[...]
    for k in range(1, g):
        img_copies[k - 1].wait_recv()
        sums = sums + img_in[k - 1]
    high = sums.astype(BF16)
    low = (sums - high.astype(F32)).astype(BF16)
    both = jnp.concatenate([high, low], axis=0)
    parts = dot_t(both[:, :width], pv[...]) + dot(both[:, width:width + heads], kq_t)
    oemb[...] = parts[:chans] + parts[chans:]
    obias[...] = sums[:, width:width + heads]
    for slot, (src, dst) in enumerate(((oemb, out_embed), (obias, out_bias))):
        copy = pltpu.make_async_copy(src, dst, store_sem.at[tiles * chans + slot])
        copy.start()
        stores.append(copy)

    for copy in sends:
        copy.wait_send()
    for k in range(1, n):
        pl.when(lax.rem(me + k, n) < heads)(stat_sends[k - 1].wait_send)
    for copy in img_copies:
        copy.wait_send()
    for copy in stores:
        copy.wait()


def body(n, g, tokens, embed, proj, query, bias, cot):
    chans, toks, width = tokens.shape
    heads = query.shape[1]
    rows = cot.shape[0]
    gather = rows % 16 == 0 and n > 1
    if not gather:
        cot = lax.all_gather(cot, "chan", axis=0, tiled=True)
    tiles = width // min(256, width)
    any_spec = pl.BlockSpec(memory_space=pl.ANY)
    dma = pltpu.SemaphoreType.DMA
    return pl.pallas_call(
        functools.partial(kernel, n, g, gather),
        out_shape=(
            jax.ShapeDtypeStruct((chans, toks, width), BF16),
            jax.ShapeDtypeStruct((chans, width), F32),
            jax.ShapeDtypeStruct((chans, heads), F32),
        ),
        in_specs=[any_spec] * 6,
        out_specs=(any_spec,) * 3,
        scratch_shapes=[
            pltpu.VMEM((chans * toks, width), BF16),
            pltpu.VMEM((chans, width), F32),
            pltpu.VMEM((width, width), BF16),
            pltpu.VMEM((width, heads), BF16),
            pltpu.VMEM(bias.shape, F32),
            pltpu.VMEM((toks, width), BF16),
            pltpu.VMEM((chans * toks, width), BF16),
            pltpu.VMEM((chans * toks, width), BF16),
            pltpu.VMEM((chans * toks, width), BF16),
            pltpu.VMEM((chans * toks, width), BF16),
            pltpu.VMEM((chans, width), F32),
            pltpu.VMEM((chans, heads), F32),
            pltpu.VMEM((heads, 3, toks), F32),
            pltpu.VMEM((n, 3, toks), F32),
            pltpu.VMEM((3, toks), F32),
            pltpu.VMEM((heads, 3, toks), F32),
            pltpu.VMEM((chans, width + 128), F32),
            pltpu.VMEM((max(1, g - 1), chans, width + 128), F32),
            dma((4 + chans + tiles,)),
            dma((tiles * chans + 2,)),
            dma((n,)),
            dma((n,)),
            dma((n,)),
            dma((n,)),
            dma((n,)),
            dma((n,)),
            dma((g,)),
            dma((g,)),
        ],
        compiler_params=pltpu.CompilerParams(
            collective_id=0, has_side_effects=True, vmem_limit_bytes=40 * 1024 * 1024
        ),
    )(tokens, embed, proj, query, bias, cot)


def solution(mesh):
    in_specs = (P("chan", "img", None), P("chan", None), P(), P(), P(), P(("img", "chan"), None))
    out_specs = (P("chan", "img", None), P("chan", None), P("chan", None))
    call = functools.partial(body, mesh.shape["chan"], mesh.shape["img"])
    return jax.shard_map(call, mesh=mesh, in_specs=in_specs, out_specs=out_specs, check_vma=False)
```

```python
import functools

import jax
import jax.numpy as jnp
from jax import lax
from jax.experimental import pallas as pl
from jax.experimental.pallas import tpu as pltpu
from jax.sharding import PartitionSpec as P

MESH = pl.DeviceIdType.MESH
F32 = jnp.float32
BF16 = jnp.bfloat16
ROWS_BY_ROWS = (((1,), (1,)), ((), ()))


def dot_t(left, right):
    return lax.dot_general(left, right, ROWS_BY_ROWS, preferred_element_type=F32)


def dot(left, right):
    return jnp.dot(left, right, preferred_element_type=F32)


def grid_of(n):
    chips = n // 2
    wide = 1
    while wide * wide * 4 <= chips:
        wide *= 2
    return chips // wide, wide


def far_first(n):
    return sorted(range(1, n), key=lambda k: -min(k, n - k))


def kernel(
    n, g, gather,
    tokens, embed, proj, query, bias, cot,
    out_grad, out_embed, out_bias,
    tok, emb, pv, kq, bia, cots, shifted, values, vgrad, acc, outv, oemb, obias,
    stat_out, stat_in, tot_out, tot_in, mean_out, mean_in, avg_out, avg_in,
    img_out, img_in, gb_out, gb_in,
    load_sem, store_sem, cot_send, cot_recv, stat_send, stat_recv, tot_send, tot_recv,
    mean_send, mean_recv, avg_send, avg_recv, img_send, img_recv, gb_send, gb_recv,
):
    chans, toks, width = tokens.shape
    heads = query.shape[0]
    depth = width // heads
    tile = min(256, width)
    tiles = width // tile
    me = lax.axis_index("chan")
    my_img = lax.axis_index("img")
    rows = cot.shape[0]

    def load(slot, src, dst):
        copy = pltpu.make_async_copy(src, dst, load_sem.at[slot])
        copy.start()
        return copy

    if gather:
        cot_load = load(0, cot, cots.at[pl.ds(pl.multiple_of(me * rows, rows), rows)])
    else:
        cot_load = load(0, cot, cots)
    small_loads = [load(1, embed, emb), load(2, bias, bia), load(3, query, kq)]
    tok_loads = [load(4 + c, tokens.at[c], tok.at[pl.ds(c * toks, toks)]) for c in range(chans)]
    proj_loads = [
        load(
            4 + chans + j,
            proj.at[:, pl.ds(j * tile, tile)],
            pv.at[:, pl.ds(j * tile, tile)],
        )
        for j in range(tiles)
    ]

    barrier = pltpu.get_barrier_semaphore()
    for k in far_first(n):
        pl.semaphore_signal(
            barrier, inc=1, device_id={"chan": lax.rem(me + k, n)}, device_id_type=MESH
        )
    for k in range(1, g):
        pl.semaphore_signal(
            barrier, inc=1, device_id={"img": lax.rem(my_img + k, g)}, device_id_type=MESH
        )

    tall, wide = grid_of(n)
    core = lax.rem(me, 2)
    my_b = lax.rem(me // 2, wide)
    my_a = me // (2 * wide)

    def index(a, b, c):
        return (a * wide + b) * 2 + c

    sends = []

    def block(i):
        return cots.at[pl.ds(pl.multiple_of(i * rows, rows), rows)]

    def send(i, to, own=False):
        copy = pltpu.make_async_remote_copy(
            src_ref=cot if own else block(i),
            dst_ref=block(i),
            send_sem=cot_send.at[len(sends)],
            recv_sem=cot_recv.at[i],
            device_id={"chan": to},
            device_id_type=MESH,
        )
        copy.start()
        sends.append(copy)

    def arrive(i):
        pltpu.make_async_remote_copy(
            src_ref=cot,
            dst_ref=block(i),
            send_sem=cot_send.at[0],
            recv_sem=cot_recv.at[i],
            device_id={"chan": me},
            device_id_type=MESH,
        ).wait_recv()

    def others_a():
        return [lax.rem(my_a + k, tall) for k in far_first(tall)]

    def others_b():
        return [lax.rem(my_b + k, wide) for k in range(1, wide)]

    pl.semaphore_wait(barrier, n - 1 + g - 1)
    mate = index(my_a, my_b, 1 - core)
    if gather:
        for a in others_a():
            send(me, index(a, my_b, core), own=True)
        for b in others_b():
            send(me, index(my_a, b, core), own=True)
        send(me, mate, own=True)

    for copy in small_loads:
        copy.wait()
    kq_t = kq[...]
    head_at = lax.broadcasted_iota(jnp.int32, (heads, width), 0) * depth
    lane_at = lax.broadcasted_iota(jnp.int32, (heads, width), 1)
    spread_f = jnp.where((lane_at >= head_at) & (lane_at < head_at + depth), 1.0, 0.0)
    spread = spread_f.astype(BF16)
    eye = lax.broadcasted_iota(jnp.int32, (heads, 128), 0) == lax.broadcasted_iota(
        jnp.int32, (heads, 128), 1
    )
    bias_all = bia[...]
    bias_at = lax.broadcasted_iota(jnp.int32, bias_all.shape, 1)

    scores = []
    for c in range(chans):
        tok_loads[c].wait()
        at = pl.ds(c * toks, toks)
        moved = (tok[at, :].astype(F32) + emb[pl.ds(c, 1), :]).astype(BF16)
        shifted[at, :] = moved
        mine = bias_at == me * chans + c
        bias_col = jnp.sum(jnp.where(mine, bias_all, 0.0), axis=1, keepdims=True)
        scores.append(dot_t(kq_t, moved) + bias_col)

    peak = functools.reduce(jnp.maximum, scores)
    stat_out[:, 0, :] = peak
    exps = [jnp.exp(s - peak) for s in scores]
    stat_out[:, 1, :] = functools.reduce(jnp.add, exps)

    def to_owners(src, dst, send_sem, recv_sem):
        copies = []
        for k in far_first(n):
            to = lax.rem(me + k, n)
            copy = pltpu.make_async_remote_copy(
                src_ref=src.at[lax.rem(to, heads)],
                dst_ref=dst.at[me],
                send_sem=send_sem.at[k],
                recv_sem=recv_sem.at[me],
                device_id={"chan": to},
                device_id_type=MESH,
            )
            pl.when(to < heads)(copy.start) if n > heads else copy.start()
            copies.append(copy)
        return copies

    def to_all(src, dst, send_sem, recv_sem):
        slot = lax.rem(me, heads)
        copies = []
        for k in far_first(n):
            copy = pltpu.make_async_remote_copy(
                src_ref=src,
                dst_ref=dst.at[slot],
                send_sem=send_sem.at[k],
                recv_sem=recv_sem.at[slot],
                device_id={"chan": lax.rem(me + k, n)},
                device_id_type=MESH,
            )
            copy.start()
            copies.append(copy)
        dst[slot] = src[...]
        return copies

    def landed(dst, recv_sem, slot):
        pltpu.make_async_remote_copy(
            src_ref=dst.at[slot],
            dst_ref=dst.at[slot],
            send_sem=load_sem.at[0],
            recv_sem=recv_sem.at[slot],
            device_id={"chan": me},
            device_id_type=MESH,
        ).wait_recv()

    def if_owner(work):
        if n == heads:
            work()
        else:
            pl.when(me < heads)(work)

    def all_landed(dst, recv_sem):
        if n == heads:
            for k in range(1, n):
                landed(dst, recv_sem, lax.rem(me + k, n))
        else:
            for h in range(heads):
                pl.when(me != h)(functools.partial(landed, dst, recv_sem, h))

    owner_sends = [(stat_out, stat_in, stat_send, stat_recv), (mean_out, mean_in, mean_send, mean_recv)]
    sent = [to_owners(*owner_sends[0])]

    def combine_totals():
        stat_in[me] = stat_out[lax.rem(me, heads)]
        for k in range(1, n):
            landed(stat_in, stat_recv, lax.rem(me + k, n))
        peaks = stat_in[:, 0, :]
        top = jnp.max(peaks, axis=0, keepdims=True)
        total = jnp.sum(stat_in[:, 1, :] * jnp.exp(peaks - top), axis=0, keepdims=True)
        tot_out[0:1, :] = top
        tot_out[1:2, :] = 1.0 / total
        for copy in to_all(tot_out, tot_in, tot_send, tot_recv):
            copy.wait_send()

    def combine_means():
        mean_in[me] = mean_out[lax.rem(me, heads)]
        for k in range(1, n):
            landed(mean_in, mean_recv, lax.rem(me + k, n))
        scale = jnp.exp(stat_in[:, 0, :] - tot_out[0:1, :])
        avg_out[...] = jnp.sum(mean_in[:, 0, :] * scale, axis=0, keepdims=True) * tot_out[1:2, :]
        for copy in to_all(avg_out, avg_in, avg_send, avg_recv):
            copy.wait_send()

    def value_tile(j):
        proj_loads[j].wait()
        cols = pl.ds(j * tile, tile)
        values[:, cols] = dot(shifted[...], pv[:, cols]).astype(BF16)

    for j in range(tiles):
        value_tile(j)
    if gather:
        for a in others_a():
            i = index(a, my_b, core)
            arrive(i)
            for b in others_b():
                send(i, index(my_a, b, core))
            send(i, mate)
    if_owner(combine_totals)
    if gather:
        for b in others_b():
            for k in range(tall):
                i = index(lax.rem(my_a + k, tall), b, core)
                arrive(i)
                send(i, mate)
    cot_load.wait()
    if gather:
        for a in range(tall):
            for b in range(wide):
                arrive(index(a, b, 1 - core))

    prob = [dot_t(spread, values[pl.ds(c * toks, toks), :] * cots[...]) for c in range(chans)]
    mean_out[:, 0, :] = functools.reduce(jnp.add, [e * p for e, p in zip(exps, prob)])
    sent.append(to_owners(*owner_sends[1]))

    all_landed(tot_in, tot_recv)
    soft = [jnp.exp(s - tot_in[:, 0, :]) * tot_in[:, 1, :] for s in scores]
    spread2 = jnp.concatenate([spread, spread], axis=0)
    for c in range(chans):
        high = soft[c].astype(BF16).astype(F32)
        mix = jnp.concatenate([high, soft[c] - high], axis=0).T.astype(BF16)
        grad = (dot(mix, spread2) * cots[...].astype(F32)).astype(BF16)
        vgrad[pl.ds(c * toks, toks), :] = grad
        img_out[pl.ds(c, 1), :] = jnp.sum(grad.astype(F32), axis=0, keepdims=True)

    def to_images(src, dst, send_sem, recv_sem):
        copies = []
        for k in range(1, g):
            copy = pltpu.make_async_remote_copy(
                src_ref=src,
                dst_ref=dst.at[k - 1],
                send_sem=send_sem.at[k],
                recv_sem=recv_sem.at[k],
                device_id={"img": lax.rem(my_img + k, g)},
                device_id_type=MESH,
            )
            copy.start()
            copies.append(copy)
        return copies

    def total_of(copies, src, dst):
        sums = src[...]
        for k, copy in enumerate(copies):
            copy.wait_recv()
            sums = sums + dst[k]
        return sums

    img_copies = to_images(img_out, img_in, img_send, img_recv)
    for j in range(tiles):
        cols = pl.ds(j * tile, tile)
        acc[:, cols] = dot_t(vgrad[...], pv[cols, :])

    if_owner(combine_means)

    def halves(sums):
        high = sums.astype(BF16)
        return jnp.concatenate([high, (sums - high.astype(F32)).astype(BF16)], axis=0)

    embed_part = dot_t(halves(total_of(img_copies, img_out, img_in)), pv[...])

    all_landed(avg_in, avg_recv)
    mean = avg_in[:, 0, :]
    slopes = []
    for c in range(chans):
        score_grad = soft[c] * (prob[c] - mean)
        slopes.append(score_grad)
        bias_sum = jnp.sum(score_grad, axis=1, keepdims=True)
        gb_out[pl.ds(c, 1), :] = jnp.sum(jnp.where(eye, bias_sum, 0.0), axis=0, keepdims=True)
    gb_copies = to_images(gb_out, gb_in, gb_send, gb_recv)

    stores = []

    def store(src, dst):
        copy = pltpu.make_async_copy(src, dst, store_sem.at[len(stores)])
        copy.start()
        stores.append(copy)

    for c in range(chans):
        at = pl.ds(c * toks, toks)
        outv[c] = (acc[at, :] + dot(slopes[c].T.astype(BF16), kq_t)).astype(BF16)
        store(outv.at[c], out_grad.at[c])

    bias_total = total_of(gb_copies, gb_out, gb_in)[:, :heads]
    parts = embed_part + dot(halves(bias_total), kq_t)
    oemb[...] = parts[:chans] + parts[chans:]
    obias[...] = bias_total
    store(oemb, out_embed)
    store(obias, out_bias)

    for copy in sends + img_copies + gb_copies:
        copy.wait_send()
    for copies in sent:
        for k, copy in zip(far_first(n), copies):
            pl.when(lax.rem(me + k, n) < heads)(copy.wait_send) if n > heads else copy.wait_send()
    for copy in stores:
        copy.wait()


def leave(*refs):
    count = len(refs) // 2
    sems = refs[-1]
    copies = [
        pltpu.make_async_copy(refs[i], refs[count + i], sems.at[i]) for i in range(count)
    ]
    for copy in copies:
        copy.start()
    for copy in copies:
        copy.wait()


def body(n, g, tokens, embed, proj, query, bias, cot):
    chans, toks, width = tokens.shape
    heads = query.shape[1]
    rows = cot.shape[0]
    gather = rows % 16 == 0 and n > 1
    if not gather:
        cot = lax.all_gather(cot, "chan", axis=0, tiled=True)
    tiles = width // min(256, width)
    any_spec = pl.BlockSpec(memory_space=pl.ANY)
    hbm_spec = pl.BlockSpec(memory_space=pltpu.HBM)
    dma = pltpu.SemaphoreType.DMA
    shapes = (
        jax.ShapeDtypeStruct((chans, toks, width), BF16),
        jax.ShapeDtypeStruct((chans, width), F32),
        jax.ShapeDtypeStruct((chans, heads), F32),
    )
    results = pl.pallas_call(
        functools.partial(kernel, n, g, gather),
        out_shape=tuple(pltpu.VMEM(x.shape, x.dtype) for x in shapes),
        in_specs=[hbm_spec] * 6,
        out_specs=(pl.BlockSpec(memory_space=pltpu.VMEM),) * 3,
        scratch_shapes=[
            pltpu.VMEM((chans * toks, width), BF16),
            pltpu.VMEM((chans, width), F32),
            pltpu.VMEM((width, width), BF16),
            pltpu.VMEM((heads, width), BF16),
            pltpu.VMEM(bias.shape[::-1], F32),
            pltpu.VMEM((toks, width), BF16),
            pltpu.VMEM((chans * toks, width), BF16),
            pltpu.VMEM((chans * toks, width), BF16),
            pltpu.VMEM((chans * toks, width), BF16),
            pltpu.VMEM((chans * toks, width), F32),
            pltpu.VMEM((chans, toks, width), BF16),
            pltpu.VMEM((chans, width), F32),
            pltpu.VMEM((chans, heads), F32),
            pltpu.VMEM((heads, 2, toks), F32),
            pltpu.VMEM((n, 2, toks), F32),
            pltpu.VMEM((2, toks), F32),
            pltpu.VMEM((heads, 2, toks), F32),
            pltpu.VMEM((heads, 1, toks), F32),
            pltpu.VMEM((n, 1, toks), F32),
            pltpu.VMEM((1, toks), F32),
            pltpu.VMEM((heads, 1, toks), F32),
            pltpu.VMEM((chans, width), F32),
            pltpu.VMEM((max(1, g - 1), chans, width), F32),
            pltpu.VMEM((chans, 128), F32),
            pltpu.VMEM((max(1, g - 1), chans, 128), F32),
            dma((4 + chans + tiles,)),
            dma((chans + 2,)),
        ]
        + [dma((n,))] * 10
        + [dma((g,))] * 4,
        compiler_params=pltpu.CompilerParams(
            collective_id=0, has_side_effects=True, vmem_limit_bytes=60 * 1024 * 1024
        ),
    )(tokens, embed, proj, query.T, bias.T, cot)
    return pl.pallas_call(
        leave,
        out_shape=shapes,
        in_specs=[any_spec] * 3,
        out_specs=(hbm_spec,) * 3,
        scratch_shapes=[dma((3,))],
        compiler_params=pltpu.CompilerParams(vmem_limit_bytes=4 * 1024 * 1024),
    )(*results)


def solution(mesh):
    in_specs = (P("chan", "img", None), P("chan", None), P(), P(), P(), P(("img", "chan"), None))
    out_specs = (P("chan", "img", None), P("chan", None), P("chan", None))
    call = functools.partial(body, mesh.shape["chan"], mesh.shape["img"])
    return jax.shard_map(call, mesh=mesh, in_specs=in_specs, out_specs=out_specs, check_vma=False)
```
